256 devices in a mesh: seq: 128 (over x, y, z), head: 2 (over core).
Axes of the slice: x: 4, y: 4, z: 8, core: 2. Of those that a mesh axis runs over, the one named last changes fastest.
Arguments:
- queries: bfloat16 [16384, 2048], P('seq', 'head'), may hold values from -0.52734375 to 0.52734375
- keys: bfloat16 [16384, 2048], P('seq', 'head'), may hold values from -0.52734375 to 0.52734375
- values: bfloat16 [16384, 2048], P('seq', 'head'), may hold values from -6 to 6
- transitions: bfloat16 [256, 16, 128, 128], P('seq', 'head'), may hold values from -0.03 to 1, as said below
- gates: float32 [256, 16], P('seq', 'head'), may hold values from 0.02 to 1
- norm_gain: float32 [128], replicated, may hold values from 0.25 to 1.75
Outputs:
- output: bfloat16 [16384, 2048], P(('seq', 'head'))
The draws below stay inside these ranges and needn't reach their ends.
Inputs may be any that keep to these rules, and one draw needn't show every extreme that they name: `transitions`: diagonal entries lie between 0.99 and 1; off-diagonal entries are small.
All inputs are finite; a program needn't handle non-finite values.
Results may differ from the reference program's by a relative error of at most 0.0095.
Values may be sent and summed in bfloat16 or wider, within the bound.
No kernel may reach another device: no remote copies, remote signals or barrier semaphores. Data moves between devices by JAX's collectives and lax.ppermute only.
A program may use at most 256 MiB of HBM per device.

```python
import math
import jax
import jax.numpy as jnp
from jax import lax

DK = 128
DV = 128
H = 16
BLOCK = 64
TOKENS = 16384
SEGMENT_TALLY = 256


def draw_transitions(key, part):
    key = jax.random.fold_in(key, 11)
    key_diag, key_off = jax.random.split(key)
    diagonal = jax.random.uniform(key_diag, (SEGMENT_TALLY, H, DK), jnp.float32, 0.99, 1.0)
    offdiag = jnp.clip(0.005 * jax.random.normal(key_off, (SEGMENT_TALLY, H, DK, DK), jnp.float32), -0.03, 0.03)
    identity_matrix = jnp.eye(DK, dtype=jnp.float32)
    matrix = offdiag * (1.0 - identity_matrix) + identity_matrix * diagonal[..., None]
    return matrix.astype(jnp.bfloat16)


def draw_gates(key, part):
    key = jax.random.fold_in(key, 12)
    key_rate, key_jit, key_pick, key_depth = jax.random.split(key, 4)
    forget_factors = jnp.exp(jax.random.uniform(key_rate, (H,), jnp.float32, math.log(0.0005), math.log(2.0)))
    stochastic_perturbation = jax.random.uniform(key_jit, (SEGMENT_TALLY, H), jnp.float32, 0.5, 1.5)
    omission_chance = jax.random.uniform(key_pick, (SEGMENT_TALLY, H), jnp.float32)
    hierarchy_height = jax.random.uniform(key_depth, (SEGMENT_TALLY, H), jnp.float32, 0.5, 0.8)
    cluster_batches = jnp.where(omission_chance < 6.0 / SEGMENT_TALLY, hierarchy_height, 1.0)
    return (jnp.exp(-forget_factors[None, :] * stochastic_perturbation) * cluster_batches).astype(jnp.float32)


def shard_levels(stream_key, extent, shards, least, high):
    level, own = 1.0, jax.random.fold_in(stream_key, 6)
    for axis_at, parts in shards:
        draws = jnp.exp(jax.random.uniform(jax.random.fold_in(own, axis_at), (parts,), jnp.float32, least / len(shards), high / len(shards)))
        level = level * jnp.repeat(draws, extent[axis_at] // parts).reshape([-1 if axis == axis_at else 1 for axis in range(len(extent))])
    return level


def gaussian(key, dims, spread, most, shards=(), held_as=jnp.bfloat16):
    array = jax.random.normal(key, dims, jnp.float32) * spread
    if len(shards) > 0:
        array = shard_levels(key, dims, shards, -0.22, 0.18) * array
    return jnp.clip(array, min=-most, max=most).astype(held_as)


def setup_inputs(seed: int = 0) -> dict:
    key_of = jax.random.split(jax.random.key(seed), 7)
    queries = gaussian(key_of[0], (TOKENS, H * DK), (DK ** -0.5), 0.52734375, ((0, 128), (1, 2)))
    keys = gaussian(key_of[1], (TOKENS, H * DK), (DK ** -0.5), 0.52734375, ((0, 128), (1, 2)))
    values = gaussian(key_of[2], (TOKENS, H * DV), 1.0, 6.0, ((0, 128), (1, 2)))
    transitions = draw_transitions(jax.random.fold_in(key_of[6], 71), 0)
    gates = draw_gates(jax.random.fold_in(key_of[6], 71), 0)
    norm_gain = jnp.clip(1.0 + 0.15 * jax.random.normal(key_of[5], (DV,), jnp.float32), 0.25, 1.75)
    return dict(queries=queries, keys=keys, values=values, transitions=transitions, gates=gates, norm_gain=norm_gain)


EPS = 1e-06

def block_output(query_blk, key_blk, value_blk, carry_state, norm_gain):
    question_vector = query_blk.astype(jnp.float32)
    key_f = key_blk.astype(jnp.float32)
    value_f = value_blk.astype(jnp.float32)
    rounded = lax.optimization_barrier(carry_state.astype(jnp.bfloat16)).astype(jnp.float32)
    carried = jnp.einsum('thd,hde->the', question_vector, rounded)
    scores = jnp.einsum('thd,shd->hts', question_vector, key_f)
    length = query_blk.shape[0]
    causal = jnp.tril(jnp.ones((length, length), dtype=bool))
    scores = jnp.where(causal[None], scores, jnp.float32(0.0))
    weights = lax.optimization_barrier(scores.astype(jnp.bfloat16)).astype(jnp.float32)
    local_term = jnp.einsum('hts,she->the', weights, value_f)
    mixed = carried + local_term
    factor = lax.rsqrt(lax.optimization_barrier(jnp.mean(mixed * mixed, axis=-1, keepdims=True)) + EPS)
    return (mixed * factor * norm_gain).astype(jnp.bfloat16)

def reference(queries, keys, values, transitions, gates, norm_gain):
    query_all = queries.reshape(SEGMENT_TALLY, BLOCK, H, DK)
    key_all = keys.reshape(SEGMENT_TALLY, BLOCK, H, DK)
    value_all = values.reshape(SEGMENT_TALLY, BLOCK, H, DV)

    def advance(carry_state, inputs):
        query_blk, key_blk, value_blk, transit_blk, gate_row = inputs
        result = block_output(query_blk, key_blk, value_blk, carry_state, norm_gain)
        full_map = transit_blk.astype(jnp.float32) * gate_row[:, None, None]
        update = jnp.einsum('thd,the->hde', key_blk.astype(jnp.float32), value_blk.astype(jnp.float32))
        new_state = jnp.einsum('hij,hjk->hik', full_map, carry_state, precision=lax.Precision.HIGHEST) + update
        return (new_state, result)
    start = jnp.zeros((H, DK, DV), jnp.float32)
    _, results = lax.scan(advance, start, (query_all, key_all, value_all, transitions, gates))
    return results.reshape(TOKENS, H * DV)
```

```python
import jax
import jax.numpy as jnp
from jax import lax
from jax.experimental import pallas as pl
from jax.experimental.pallas import tpu as pltpu
from jax.sharding import PartitionSpec as P

EPS = 1e-06
D = 128
ROWS = 2 * D + 16
F32 = jnp.float32
BF16 = jnp.bfloat16
VMEM = pl.BlockSpec(memory_space=pltpu.VMEM)
SMEM = pl.BlockSpec(memory_space=pltpu.SMEM)


def dot(a, b, ca, cb):
    return lax.dot_general(a, b, (((ca,), (cb,)), ((), ())), preferred_element_type=F32)


def eye_mask():
    return lax.broadcasted_iota(jnp.int32, (D, D), 0) == lax.broadcasted_iota(
        jnp.int32, (D, D), 1
    )


def split(matrix, eye):
    matrix = matrix.astype(F32)
    row = jnp.sum(jnp.where(eye, matrix, 0.0), axis=0, keepdims=True)
    return row, jnp.where(eye, 0.0, matrix).astype(BF16)


def pack(ref, at, matrix, state, eye):
    row, rest = split(matrix, eye)
    high = row.astype(BF16)
    low = (row - high.astype(F32)).astype(BF16)
    ref[(*at, pl.ds(0, D))] = rest
    ref[(*at, pl.ds(D, D))] = state.astype(BF16)
    tail = lax.broadcasted_iota(jnp.int32, (16, D), 0)
    both = jnp.where(tail == 0, high.astype(F32), jnp.where(tail == 1, low.astype(F32), 0.0))
    ref[(*at, pl.ds(2 * D, 16))] = both.astype(BF16)


def unpack(ref, at):
    rest = ref[(*at, pl.ds(0, D))]
    state = ref[(*at, pl.ds(D, D))].astype(F32)
    tail = ref[(*at, pl.ds(2 * D, 16))].astype(F32)
    row = tail[0:1] + tail[1:2]
    return row, rest, state


def local_compose(trans_ref, gate_ref, key_ref, value_ref, wire_ref):
    eye = eye_mask()
    heads = trans_ref.shape[1]
    rows = key_ref.shape[0] // 2
    for h in range(heads):
        cols = pl.ds(h * D, D)
        g0 = gate_ref[0, h]
        g1 = gate_ref[1, h]
        row0, rest0 = split(trans_ref[0, h], eye)
        row1, rest1 = split(trans_ref[1, h], eye)
        a1 = trans_ref[1, h]
        upd0 = dot(value_ref[pl.ds(0, rows), cols], key_ref[pl.ds(0, rows), cols], 0, 0)
        upd1 = dot(value_ref[pl.ds(rows, rows), cols], key_ref[pl.ds(rows, rows), cols], 0, 0)
        matrix = (g0 * g1) * (a1.astype(F32) * row0 + dot(a1, rest0, 1, 0))
        state = g1 * (upd0 * row1 + dot(upd0.astype(BF16), rest1, 1, 1)) + upd1
        pack(wire_ref, (h,), matrix, state, eye)


def group_prefix(wire_ref, pre_ref, total_ref):
    eye = eye_mask()
    count = wire_ref.shape[0]
    run = jnp.concatenate([eye.astype(F32), jnp.zeros((D, D), F32)], axis=0)
    for z in range(count):
        row, rest, state = unpack(wire_ref, (z,))
        pack(pre_ref, (z,), run[:D], run[D:], eye)
        run = run * row + dot(run.astype(BF16), rest, 1, 1)
        run = run + jnp.concatenate([jnp.zeros((D, D), F32), state], axis=0)
    pack(total_ref, (), run[:D], run[D:], eye)


def ring_prefix(axis, stride, own_ref, a_ref, b_ref, c_ref, pre_ref, total_ref, sorted_ref):
    eye = eye_mask()
    me = lax.rem(lax.axis_index(axis) // stride, 4)
    for d, ref in enumerate((own_ref, a_ref, b_ref, c_ref)):
        sorted_ref[lax.rem(me + 4 - d, 4)] = ref[...]
    run = jnp.concatenate([eye.astype(F32), jnp.zeros((D, D), F32)], axis=0)
    before = run
    for p in range(4):
        if p:
            before = jnp.where(me == p, run, before)
        row, rest, state = unpack(sorted_ref, (p,))
        run = run * row + dot(run.astype(BF16), rest, 1, 0)
        run = run + jnp.concatenate([jnp.zeros((D, D), F32), state], axis=0)
    pack(pre_ref, (), before[:D], before[D:], eye)
    pack(total_ref, (), run[:D], run[D:], eye)


def enter_states(
    axis, stride, own_ref, a_ref, b_ref, c_ref, outer_ref, pre_ref, state_ref, sorted_ref
):
    me = lax.rem(lax.axis_index(axis) // stride, 4)
    for d, ref in enumerate((own_ref, a_ref, b_ref, c_ref)):
        sorted_ref[lax.rem(me + 4 - d, 4)] = ref[...]

    def apply(run, ref, at):
        row, rest, state = unpack(ref, at)
        return run * row + dot(run.astype(BF16), rest, 1, 0) + state

    run = jnp.zeros((D, D), F32)
    before = run
    for p in range(3):
        run = apply(run, sorted_ref, (p,))
        before = jnp.where(me == p + 1, run, before)
    run = apply(before, outer_ref, ())
    for z in range(pre_ref.shape[0]):
        state_ref[z] = apply(run, pre_ref, (z,)).astype(BF16)


def outputs(
    query_ref, key_ref, value_ref, trans_ref, gate_ref, state_ref, gain_ref, out_ref
):
    eye = eye_mask()
    heads = trans_ref.shape[1]
    rows = key_ref.shape[0] // 2
    me = lax.axis_index("head")
    causal = lax.broadcasted_iota(jnp.int32, (rows, rows), 0) >= lax.broadcasted_iota(
        jnp.int32, (rows, rows), 1
    )
    gain = gain_ref[...]
    for h in range(heads):
        cols = pl.ds(h * D, D)
        entering = state_ref[h]
        row0, rest0 = split(trans_ref[0, h], eye)
        upd0 = dot(value_ref[pl.ds(0, rows), cols], key_ref[pl.ds(0, rows), cols], 0, 0)
        later = gate_ref[0, h] * (entering.astype(F32) * row0 + dot(entering, rest0, 1, 1)) + upd0
        for c, state in enumerate((entering, later.astype(BF16))):
            here = pl.ds(c * rows, rows)
            query = query_ref[here, cols]
            weights = jnp.where(causal, dot(query, key_ref[here, cols], 1, 1), 0.0).astype(BF16)
            mixed = dot(query, state, 1, 1) + dot(weights, value_ref[here, cols], 1, 0)
            factor = lax.rsqrt(jnp.mean(mixed * mixed, axis=-1, keepdims=True) + EPS)
            out_ref[lax.rem(me + c, 2), :, cols] = (mixed * factor * gain).astype(BF16)


def shards(queries, keys, values, transitions, gates, norm_gain):
    heads = transitions.shape[1]
    count = lax.axis_size("seq")
    lines = [[g * 8 + z for z in range(8)] for g in range(count // 8)]

    def around(stride, d):
        out = []
        for s in range(count):
            at = s // stride % 4
            out.append((s, s + ((at + d) % 4 - at) * stride))
        return out

    wire = pl.pallas_call(
        local_compose,
        out_shape=jax.ShapeDtypeStruct((heads, ROWS, D), BF16),
        in_specs=[VMEM, SMEM, VMEM, VMEM],
        out_specs=VMEM,
        name="local_compose",
    )(transitions, gates, keys, values)
    with jax.named_scope("to_owners"):
        wire = lax.all_to_all(wire, "seq", 0, 0, axis_index_groups=lines, tiled=True)
    one = jax.ShapeDtypeStruct((ROWS, D), BF16)
    pre, total = pl.pallas_call(
        group_prefix,
        out_shape=[jax.ShapeDtypeStruct(wire.shape, BF16), one],
        in_specs=[VMEM],
        out_specs=[VMEM, VMEM],
        name="group_prefix",
    )(wire)
    with jax.named_scope("along_y"):
        others = [lax.ppermute(total, "seq", around(8, d)) for d in (1, 2, 3)]
    outer, total = pl.pallas_call(
        lambda *refs: ring_prefix("seq", 8, *refs),
        out_shape=[one, one],
        in_specs=[VMEM] * 4,
        out_specs=[VMEM, VMEM],
        scratch_shapes=[pltpu.VMEM((4, ROWS, D), BF16)],
        name="ring_prefix",
    )(total, *others)
    with jax.named_scope("along_x"):
        others = [lax.ppermute(total, "seq", around(32, d)) for d in (1, 2, 3)]
    states = pl.pallas_call(
        lambda *refs: enter_states("seq", 32, *refs),
        out_shape=jax.ShapeDtypeStruct((wire.shape[0], D, D), BF16),
        in_specs=[VMEM] * 6,
        out_specs=VMEM,
        scratch_shapes=[pltpu.VMEM((4, ROWS, D), BF16)],
        name="enter_states",
    )(total, *others, outer, pre)
    with jax.named_scope("from_owners"):
        states = lax.all_to_all(states, "seq", 0, 0, axis_index_groups=lines, tiled=True)
    rows = queries.shape[0] // 2
    out = pl.pallas_call(
        outputs,
        out_shape=jax.ShapeDtypeStruct((2, rows, heads * D), BF16),
        in_specs=[VMEM, VMEM, VMEM, VMEM, SMEM, VMEM, VMEM],
        out_specs=VMEM,
        name="outputs",
    )(queries, keys, values, transitions, gates, states, norm_gain.reshape(1, D))
    with jax.named_scope("to_tokens"):
        other = lax.ppermute(out[1], "head", [(0, 1), (1, 0)])
    first = lax.axis_index("head") == 0
    return jnp.concatenate(
        [jnp.where(first, out[0], other), jnp.where(first, other, out[0])], axis=1
    )


def solution(mesh):
    placed = (
        P("seq", "head"),
        P("seq", "head"),
        P("seq", "head"),
        P("seq", "head", None, None),
        P("seq", "head"),
        P(),
    )
    return jax.shard_map(
        shards, mesh=mesh, in_specs=placed, out_specs=P(("seq", "head"), None), check_vma=False
    )
```

```python
import jax
import jax.numpy as jnp
from jax import lax
from jax.experimental import pallas as pl
from jax.experimental.pallas import tpu as pltpu
from jax.sharding import PartitionSpec as P

EPS = 1e-06
D = 128
ROWS = 2 * D + 16
F32 = jnp.float32
BF16 = jnp.bfloat16
VMEM = pl.BlockSpec(memory_space=pltpu.VMEM)
PLAIN = pl.BlockSpec(memory_space=pltpu.VMEM)
SMEM = pl.BlockSpec(memory_space=pltpu.SMEM)
ANY = pl.BlockSpec(memory_space=pl.ANY)


def dot(a, b, ca, cb):
    return lax.dot_general(a, b, (((ca,), (cb,)), ((), ())), preferred_element_type=F32)


def eye_mask():
    return lax.broadcasted_iota(jnp.int32, (D, D), 0) == lax.broadcasted_iota(
        jnp.int32, (D, D), 1
    )


def split(matrix, eye):
    matrix = matrix.astype(F32)
    row = jnp.sum(jnp.where(eye, matrix, 0.0), axis=0, keepdims=True)
    return row, jnp.where(eye, 0.0, matrix).astype(BF16)


def pack(ref, at, both, eye):
    row, rest = split(both[:D], eye)
    high = row.astype(BF16)
    low = (row - high.astype(F32)).astype(BF16)
    ref[(*at, pl.ds(0, D))] = rest
    ref[(*at, pl.ds(D, D))] = both[D:].astype(BF16)
    place = lax.broadcasted_iota(jnp.int32, (16, D), 0)
    tail = jnp.where(place == 0, high.astype(F32), jnp.where(place == 1, low.astype(F32), 0.0))
    ref[(*at, pl.ds(2 * D, 16))] = tail.astype(BF16)


def unpack(ref, at=()):
    tail = ref[(*at, pl.ds(2 * D, 16))].astype(F32)
    rest = ref[(*at, pl.ds(0, D))]
    return tail[0:1] + tail[1:2], rest, ref[(*at, pl.ds(D, D))].astype(F32)


def dense(parts, eye):
    row, rest, state = parts
    return jnp.concatenate([jnp.where(eye, row, rest.astype(F32)), state], axis=0)


def divide(both, eye):
    return (*split(both[:D], eye), both[D:])


def then(both, parts):
    row, rest, state = parts
    after = both * row + dot(both.astype(BF16), rest, 1, 0)
    return jnp.concatenate([after[:D], after[D:] + state], axis=0)


def advance(state, parts):
    row, rest, add = parts
    return state * row + dot(state.astype(BF16), rest, 1, 0) + add


def local_compose(
    trans_hbm, gate_ref, key_hbm, value_hbm, wire_ref, trans_ref, key_ref, value_ref, sems
):
    heads = range(trans_ref.shape[1])
    rows = key_ref.shape[0] // 2
    pairs = (
        (key_hbm, key_ref),
        (value_hbm, value_ref),
        (trans_hbm.at[1], trans_ref.at[1]),
        (trans_hbm.at[0], trans_ref.at[0]),
    )
    copies = [pltpu.make_async_copy(*pair, sems.at[i]) for i, pair in enumerate(pairs)]
    for copy in copies:
        copy.start()
    eye = eye_mask()
    copies[0].wait()
    copies[1].wait()

    def update(c, h):
        here = (pl.ds(c * rows, rows), pl.ds(h * D, D))
        return dot(value_ref[here], key_ref[here], 0, 0)

    updates = [(update(0, h), update(1, h)) for h in heads]
    copies[2].wait()
    states = []
    for h in heads:
        upd0, upd1 = updates[h]
        high = upd0.astype(BF16)
        low = (upd0 - high.astype(F32)).astype(BF16)
        moved = dot(jnp.concatenate([high, low], axis=0), trans_ref[1, h], 1, 1)
        states.append(gate_ref[1, h] * (moved[:D] + moved[D:]) + upd1)
    copies[3].wait()
    for h in heads:
        matrix = dot(trans_ref[0, h], trans_ref[1, h], 0, 1)
        matrix = (gate_ref[0, h] * gate_ref[1, h]) * matrix
        pack(wire_ref, (h,), jnp.concatenate([matrix, states[h]], axis=0), eye)


def line_total(wire_ref, total_ref):
    eye = eye_mask()
    count = wire_ref.shape[0]
    runs = [
        then(dense(unpack(wire_ref, (z,)), eye), unpack(wire_ref, (z + 1,)))
        for z in range(0, count, 2)
    ]
    while len(runs) > 1:
        runs = [then(runs[i], divide(runs[i + 1], eye)) for i in range(0, len(runs), 2)]
    pack(total_ref, (), runs[0], eye)


def line_before(wire_ref, gain_in_ref, pre_ref, gain_ref):
    gain_ref[...] = gain_in_ref[...]
    eye = eye_mask()
    run = jnp.concatenate([eye.astype(F32), jnp.zeros((D, D), F32)], axis=0)
    for z in range(wire_ref.shape[0]):
        pack(pre_ref, (z,), run, eye)
        if z == 0:
            run = dense(unpack(wire_ref, (0,)), eye)
        elif z < wire_ref.shape[0] - 1:
            run = then(run, unpack(wire_ref, (z,)))


def sort_ring(stride, refs, sorted_ref):
    me = lax.rem(lax.axis_index("seq") // stride, 4)
    for d, ref in zip((0, 3, 1, 2), refs):
        sorted_ref[lax.rem(me + 4 - d, 4)] = ref[...]
    return me


def plane_total(own_ref, a_ref, b_ref, c_ref, total_ref, sorted_ref):
    eye = eye_mask()
    sort_ring(8, (own_ref, a_ref, b_ref, c_ref), sorted_ref)
    one = then(dense(unpack(sorted_ref, (0,)), eye), unpack(sorted_ref, (1,)))
    two = then(dense(unpack(sorted_ref, (2,)), eye), unpack(sorted_ref, (3,)))
    pack(total_ref, (), then(one, divide(two, eye)), eye)


def plane_before(own_ref, a_ref, b_ref, c_ref, pre_ref, sorted_ref):
    eye = eye_mask()
    me = sort_ring(8, (own_ref, a_ref, b_ref, c_ref), sorted_ref)
    before = jnp.concatenate([eye.astype(F32), jnp.zeros((D, D), F32)], axis=0)
    run = dense(unpack(sorted_ref, (0,)), eye)
    before = jnp.where(me == 1, run, before)
    for y in (1, 2):
        run = then(run, unpack(sorted_ref, (y,)))
        before = jnp.where(me == y + 1, run, before)
    pack(pre_ref, (), before, eye)


def enter_states(own_ref, a_ref, b_ref, c_ref, plane_ref, line_ref, state_ref, sorted_ref):
    me = sort_ring(32, (own_ref, a_ref, b_ref, c_ref), sorted_ref)
    run = sorted_ref[0, pl.ds(D, D)].astype(F32)
    before = jnp.where(me == 1, run, 0.0)
    for x in (1, 2):
        run = advance(run, unpack(sorted_ref, (x,)))
        before = jnp.where(me == x + 1, run, before)
    run = advance(before, unpack(plane_ref))
    for z in range(line_ref.shape[0]):
        state_ref[z] = advance(run, unpack(line_ref, (z,))).astype(BF16)


def normed_block(block, query_ref, key_ref, value_ref, state_ref, gain_ref, out_ref):
    rows = key_ref.shape[0] // 2
    here = pl.ds(pl.multiple_of(block * rows, rows), rows)
    causal = lax.broadcasted_iota(jnp.int32, (rows, rows), 0) >= lax.broadcasted_iota(
        jnp.int32, (rows, rows), 1
    )
    gain = gain_ref[...]
    heads = range(state_ref.shape[0])
    cols = [pl.ds(h * D, D) for h in heads]
    scores = [dot(query_ref[here, c], key_ref[here, c], 1, 1) for c in cols]
    weights = [jnp.where(causal, x, 0.0).astype(BF16) for x in scores]
    mixed = [
        dot(query_ref[here, c], state_ref[h], 1, 1) + dot(w, value_ref[here, c], 1, 0)
        for h, c, w in zip(heads, cols, weights)
    ]
    for h in heads:
        mean = jnp.mean(mixed[h] * mixed[h], axis=-1, keepdims=True)
        out_ref(h, (mixed[h] * lax.rsqrt(mean + EPS) * gain).astype(BF16))


def sent_outputs(
    query_ref, key_ref, value_ref, trans_ref, gate_ref, state_ref, gain_ref,
    send_ref, kept_ref, used_ref,
):
    rows = key_ref.shape[0] // 2
    me = lax.axis_index("head")
    for h in range(state_ref.shape[0]):
        cols = pl.ds(h * D, D)
        entering = state_ref[h]
        upd = dot(value_ref[pl.ds(0, rows), cols], key_ref[pl.ds(0, rows), cols], 0, 0)
        later = gate_ref[0, h] * dot(entering, trans_ref[0, h], 1, 1) + upd
        first = entering.astype(F32)
        used_ref[h] = jnp.where(me == 0, later, first).astype(BF16)
        kept_ref[h] = jnp.where(me == 0, first, later).astype(BF16)

    def write(h, value):
        send_ref[:, pl.ds(h * D, D)] = value

    normed_block(1 - me, query_ref, key_ref, value_ref, used_ref, gain_ref, write)


def kept_outputs(query_ref, key_ref, value_ref, state_ref, gain_ref, out_ref):
    me = lax.axis_index("head")
    start = me * (state_ref.shape[0] * D)

    def write(h, value):
        out_ref[:, pl.ds(pl.multiple_of(start + h * D, D), D)] = value

    normed_block(me, query_ref, key_ref, value_ref, state_ref, gain_ref, write)


def call(kernel, outs, *operands, scratch=(), flops=0, specs=None):
    shapes = [
        jax.ShapeDtypeStruct(*out[:2]) if len(out) > 2 else pltpu.VMEM(*out) for out in outs
    ]
    specs = specs or [VMEM] * len(operands)
    operands = [
        pltpu.with_memory_space_constraint(x, pltpu.VMEM) if spec is VMEM else x
        for x, spec in zip(operands, specs)
    ]
    return pl.pallas_call(
        kernel,
        out_shape=shapes,
        in_specs=specs,
        out_specs=[VMEM] * len(outs),
        scratch_shapes=scratch,
        cost_estimate=pl.CostEstimate(flops=flops, bytes_accessed=1 << 20, transcendentals=0),
        name=kernel.__name__,
    )(*operands)


def shards(queries, keys, values, transitions, gates, norm_gain):
    heads = transitions.shape[1]
    count = lax.axis_size("seq")
    tokens = queries.shape[0]
    lines = [[g * 8 + z for z in range(8)] for g in range(count // 8)]
    line = ((heads, ROWS, D), BF16)
    one = ((ROWS, D), BF16)
    ring = [pltpu.VMEM((4, ROWS, D), BF16)]

    def around(total, stride):
        out = []
        for d in (3, 1, 2):
            pairs = []
            for s in range(count):
                at = s // stride % 4
                pairs.append((s, s + ((at + d) % 4 - at) * stride))
            out.append(lax.ppermute(total, "seq", pairs))
        return lax.optimization_barrier(out)

    (wire,) = call(
        local_compose, [line], transitions, gates, keys, values, specs=[ANY, SMEM, ANY, ANY],
        scratch=[
            pltpu.VMEM(transitions.shape, BF16),
            pltpu.VMEM(keys.shape, BF16),
            pltpu.VMEM(values.shape, BF16),
            pltpu.SemaphoreType.DMA((4,)),
        ],
    )
    with jax.named_scope("to_owners"):
        wire = lax.all_to_all(wire, "seq", 0, 0, axis_index_groups=lines, tiled=True)
    (total,) = call(line_total, [one], wire)
    with jax.named_scope("along_y"):
        others = around(total, 8)
    line_pre, gain = call(
        line_before, [line, ((1, D), F32)], wire, norm_gain.reshape(1, D), specs=[VMEM, PLAIN]
    )
    (whole,) = call(plane_total, [one], total, *others, scratch=ring)
    with jax.named_scope("along_x"):
        planes = around(whole, 32)
    (plane_pre,) = call(plane_before, [one], total, *others, scratch=ring)
    (states,) = call(
        enter_states, [((heads, D, D), BF16)], whole, *planes, plane_pre, line_pre, scratch=ring
    )
    with jax.named_scope("from_owners"):
        states = lax.all_to_all(states, "seq", 0, 0, axis_index_groups=lines, tiled=True)
    half = (tokens // 2, heads * D)
    send, kept = call(
        sent_outputs,
        [(half, BF16), ((heads, D, D), BF16)],
        queries, keys, values, transitions, gates, states, gain,
        specs=[VMEM] * 4 + [SMEM] + [VMEM] * 2,
        scratch=[pltpu.VMEM((heads, D, D), BF16)],
    )
    with jax.named_scope("to_tokens"):
        other = lax.ppermute(send, "head", [(0, 1), (1, 0)])
    (out,) = call(
        kept_outputs, [((tokens // 2, 2 * heads * D), BF16, "hbm")],
        queries, keys, values, kept, gain,
    )
    there = (1 - lax.axis_index("head")) * (heads * D)
    return lax.dynamic_update_slice(out, other, (0, there))


def solution(mesh):
    placed = (
        P("seq", "head"),
        P("seq", "head"),
        P("seq", "head"),
        P("seq", "head", None, None),
        P("seq", "head"),
        P(),
    )
    return jax.shard_map(
        shards, mesh=mesh, in_specs=placed, out_specs=P(("seq", "head"), None), check_vma=False
    )
```

```python
import jax
import jax.numpy as jnp
from jax import lax
from jax.experimental import pallas as pl
from jax.experimental.pallas import tpu as pltpu
from jax.sharding import PartitionSpec as P

EPS = 1e-06
D = 128
ROWS = 2 * D + 16
F32 = jnp.float32
BF16 = jnp.bfloat16
VMEM = pl.BlockSpec(memory_space=pltpu.VMEM)
PLAIN = pl.BlockSpec(memory_space=pltpu.VMEM)
ANY = pl.BlockSpec(memory_space=pl.ANY)


def dot(a, b, ca, cb):
    return lax.dot_general(a, b, (((ca,), (cb,)), ((), ())), preferred_element_type=F32)


def eye_mask():
    return lax.broadcasted_iota(jnp.int32, (D, D), 0) == lax.broadcasted_iota(
        jnp.int32, (D, D), 1
    )


def split(matrix, eye):
    matrix = matrix.astype(F32)
    row = jnp.sum(jnp.where(eye, matrix, 0.0), axis=0, keepdims=True)
    return row, jnp.where(eye, 0.0, matrix).astype(BF16)


def pack(ref, at, both, eye):
    row, rest = split(both[:D], eye)
    high = row.astype(BF16)
    low = (row - high.astype(F32)).astype(BF16)
    ref[(*at, pl.ds(0, D))] = rest
    ref[(*at, pl.ds(D, D))] = both[D:].astype(BF16)
    place = lax.broadcasted_iota(jnp.int32, (16, D), 0)
    tail = jnp.where(place == 0, high.astype(F32), jnp.where(place == 1, low.astype(F32), 0.0))
    ref[(*at, pl.ds(2 * D, 16))] = tail.astype(BF16)


def unpack(ref, at=()):
    tail = ref[(*at, pl.ds(2 * D, 16))].astype(F32)
    rest = ref[(*at, pl.ds(0, D))]
    return tail[0:1] + tail[1:2], rest, ref[(*at, pl.ds(D, D))].astype(F32)


def dense(parts, eye):
    row, rest, state = parts
    return jnp.concatenate([jnp.where(eye, row, rest.astype(F32)), state], axis=0)


def divide(both, eye):
    return (*split(both[:D], eye), both[D:])


def then(both, parts):
    row, rest, state = parts
    after = both * row + dot(both.astype(BF16), rest, 1, 0)
    return jnp.concatenate([after[:D], after[D:] + state], axis=0)


def advance(state, parts):
    row, rest, add = parts
    return state * row + dot(state.astype(BF16), rest, 1, 0) + add


def local_compose(
    trans_hbm, gate_hbm, key_hbm, value_hbm, wire_ref, trans_ref, gate_ref, key_ref, value_ref, sems
):
    heads = range(trans_ref.shape[1])
    rows = key_ref.shape[0] // 2
    pairs = (
        (gate_hbm, gate_ref),
        (key_hbm, key_ref),
        (value_hbm, value_ref),
        (trans_hbm, trans_ref),
    )
    copies = [pltpu.make_async_copy(*pair, sems.at[i]) for i, pair in enumerate(pairs)]
    for copy in copies:
        copy.start()
    eye = eye_mask()
    copies[1].wait()
    copies[2].wait()

    def update(c, h):
        here = (pl.ds(c * rows, rows), pl.ds(h * D, D))
        return dot(value_ref[here], key_ref[here], 0, 0)

    updates = [(update(0, h).astype(BF16), update(1, h)) for h in heads]
    copies[0].wait()
    copies[3].wait()
    for h in heads:
        first, second = updates[h]
        a1 = trans_ref[1, h]
        state = gate_ref[1, h] * dot(first, a1, 1, 1) + second
        matrix = (gate_ref[0, h] * gate_ref[1, h]) * dot(trans_ref[0, h], a1, 0, 1)
        pack(wire_ref, (h,), jnp.concatenate([matrix, state], axis=0), eye)


def line_total(wire_ref, total_ref):
    eye = eye_mask()
    count = wire_ref.shape[0]
    runs = [
        then(dense(unpack(wire_ref, (z,)), eye), unpack(wire_ref, (z + 1,)))
        for z in range(0, count, 2)
    ]
    while len(runs) > 1:
        runs = [then(runs[i], divide(runs[i + 1], eye)) for i in range(0, len(runs), 2)]
    pack(total_ref, (), runs[0], eye)


def line_before(wire_ref, gain_in_ref, gate_in_ref, pre_ref, gain_ref, gate_ref):
    gain_ref[...] = gain_in_ref[...]
    for h in range(gate_ref.shape[0]):
        gate_ref[pl.ds(h, 1)] = jnp.broadcast_to(gate_in_ref[0:1, h : h + 1], (1, D))
    eye = eye_mask()
    run = jnp.concatenate([eye.astype(F32), jnp.zeros((D, D), F32)], axis=0)
    for z in range(wire_ref.shape[0]):
        pack(pre_ref, (z,), run, eye)
        if z == 0:
            run = dense(unpack(wire_ref, (0,)), eye)
        elif z < wire_ref.shape[0] - 1:
            run = then(run, unpack(wire_ref, (z,)))


def sort_ring(stride, refs, sorted_ref):
    me = lax.rem(lax.axis_index("seq") // stride, 4)
    for d, ref in zip((0, 2, 1, 3), refs):
        sorted_ref[lax.rem(me + 4 - d, 4)] = ref[...]
    return me


def plane_total(own_ref, a_ref, b_ref, c_ref, total_ref, sorted_ref):
    eye = eye_mask()
    sort_ring(8, (own_ref, a_ref, b_ref, c_ref), sorted_ref)
    one = then(dense(unpack(sorted_ref, (0,)), eye), unpack(sorted_ref, (1,)))
    two = then(dense(unpack(sorted_ref, (2,)), eye), unpack(sorted_ref, (3,)))
    pack(total_ref, (), then(one, divide(two, eye)), eye)


def plane_before(own_ref, a_ref, b_ref, c_ref, pre_ref, sorted_ref):
    eye = eye_mask()
    me = sort_ring(8, (own_ref, a_ref, b_ref, c_ref), sorted_ref)
    before = jnp.concatenate([eye.astype(F32), jnp.zeros((D, D), F32)], axis=0)
    run = dense(unpack(sorted_ref, (0,)), eye)
    before = jnp.where(me == 1, run, before)
    for y in (1, 2):
        run = then(run, unpack(sorted_ref, (y,)))
        before = jnp.where(me == y + 1, run, before)
    pack(pre_ref, (), before, eye)


def enter_states(own_ref, a_ref, b_ref, c_ref, plane_ref, line_ref, state_ref, sorted_ref):
    me = sort_ring(32, (own_ref, a_ref, b_ref, c_ref), sorted_ref)
    run = sorted_ref[0, pl.ds(D, D)].astype(F32)
    before = jnp.where(me == 1, run, 0.0)
    for x in (1, 2):
        run = advance(run, unpack(sorted_ref, (x,)))
        before = jnp.where(me == x + 1, run, before)
    run = advance(before, unpack(plane_ref))
    for z in range(line_ref.shape[0]):
        state_ref[z] = advance(run, unpack(line_ref, (z,))).astype(BF16)


def normed_block(block, query_ref, key_ref, value_ref, state_ref, gain_ref, out_ref):
    rows = key_ref.shape[0] // 2
    here = pl.ds(pl.multiple_of(block * rows, rows), rows)
    causal = lax.broadcasted_iota(jnp.int32, (rows, rows), 0) >= lax.broadcasted_iota(
        jnp.int32, (rows, rows), 1
    )
    gain = gain_ref[...]
    heads = range(state_ref.shape[0])
    cols = [pl.ds(h * D, D) for h in heads]
    scores = [dot(query_ref[here, c], key_ref[here, c], 1, 1) for c in cols]
    weights = [jnp.where(causal, x, 0.0).astype(BF16) for x in scores]
    mixed = [
        dot(query_ref[here, c], state_ref[h], 1, 1) + dot(w, value_ref[here, c], 1, 0)
        for h, c, w in zip(heads, cols, weights)
    ]
    for h in heads:
        mean = jnp.mean(mixed[h] * mixed[h], axis=-1, keepdims=True)
        out_ref(h, (mixed[h] * lax.rsqrt(mean + EPS) * gain).astype(BF16))


def sent_outputs(
    query_ref, key_ref, value_ref, trans_ref, gate_ref, state_ref, gain_ref,
    send_ref, kept_ref, used_ref,
):
    rows = key_ref.shape[0] // 2
    me = lax.axis_index("head")
    for h in range(state_ref.shape[0]):
        cols = pl.ds(h * D, D)
        entering = state_ref[h]
        upd = dot(value_ref[pl.ds(0, rows), cols], key_ref[pl.ds(0, rows), cols], 0, 0)
        later = gate_ref[pl.ds(h, 1)] * dot(entering, trans_ref[0, h], 1, 1) + upd
        first = entering.astype(F32)
        used_ref[h] = jnp.where(me == 0, later, first).astype(BF16)
        kept_ref[h] = jnp.where(me == 0, first, later).astype(BF16)

    def write(h, value):
        send_ref[:, pl.ds(h * D, D)] = value

    normed_block(1 - me, query_ref, key_ref, value_ref, used_ref, gain_ref, write)


def kept_outputs(query_ref, key_ref, value_ref, state_ref, gain_ref, out_hbm, half_ref, sem):
    me = lax.axis_index("head")
    width = half_ref.shape[1]

    def write(h, value):
        half_ref[:, pl.ds(h * D, D)] = value

    normed_block(me, query_ref, key_ref, value_ref, state_ref, gain_ref, write)
    here = pl.ds(pl.multiple_of(me * width, width), width)
    copy = pltpu.make_async_copy(half_ref, out_hbm.at[:, here], sem)
    copy.start()
    copy.wait()


def call(kernel, outs, *operands, scratch=(), flops=0, specs=None):
    shapes = [
        jax.ShapeDtypeStruct(*out[:2]) if len(out) > 2 else pltpu.VMEM(*out) for out in outs
    ]
    specs = specs or [VMEM] * len(operands)
    operands = [
        pltpu.with_memory_space_constraint(x, pltpu.VMEM) if spec is VMEM else x
        for x, spec in zip(operands, specs)
    ]
    return pl.pallas_call(
        kernel,
        out_shape=shapes,
        in_specs=specs,
        out_specs=[ANY if len(out) > 2 else VMEM for out in outs],
        scratch_shapes=scratch,
        cost_estimate=pl.CostEstimate(flops=flops, bytes_accessed=1 << 20, transcendentals=0),
        name=kernel.__name__,
    )(*operands)


def shards(queries, keys, values, transitions, gates, norm_gain):
    heads = transitions.shape[1]
    count = lax.axis_size("seq")
    tokens = queries.shape[0]
    lines = [[g * 8 + z for z in range(8)] for g in range(count // 8)]
    line = ((heads, ROWS, D), BF16)
    one = ((ROWS, D), BF16)
    ring = [pltpu.VMEM((4, ROWS, D), BF16)]

    def around(total, stride):
        out = []
        for d in (2, 1, 3):
            pairs = []
            for s in range(count):
                at = s // stride % 4
                pairs.append((s, s + ((at + d) % 4 - at) * stride))
            out.append(lax.ppermute(total, "seq", pairs))
        return lax.optimization_barrier(out)

    (wire,) = call(
        local_compose, [line], transitions, gates, keys, values, specs=[ANY] * 4,
        scratch=[
            pltpu.VMEM(transitions.shape, BF16),
            pltpu.SMEM(gates.shape, F32),
            pltpu.VMEM(keys.shape, BF16),
            pltpu.VMEM(values.shape, BF16),
            pltpu.SemaphoreType.DMA((4,)),
        ],
    )
    with jax.named_scope("to_owners"):
        wire = lax.all_to_all(wire, "seq", 0, 0, axis_index_groups=lines, tiled=True)
    (total,) = call(line_total, [one], wire)
    with jax.named_scope("along_y"):
        others = around(total, 8)
    line_pre, gain, gate = call(
        line_before, [line, ((1, D), F32), ((heads, D), F32)],
        wire, norm_gain.reshape(1, D), gates, specs=[VMEM, PLAIN, PLAIN],
    )
    (whole,) = call(plane_total, [one], total, *others, scratch=ring)
    with jax.named_scope("along_x"):
        planes = around(whole, 32)
    (plane_pre,) = call(plane_before, [one], total, *others, scratch=ring)
    (states,) = call(
        enter_states, [((heads, D, D), BF16)], whole, *planes, plane_pre, line_pre, scratch=ring
    )
    with jax.named_scope("from_owners"):
        states = lax.all_to_all(states, "seq", 0, 0, axis_index_groups=lines, tiled=True)
    half = (tokens // 2, heads * D)
    send, kept = call(
        sent_outputs,
        [(half, BF16), ((heads, D, D), BF16)],
        queries, keys, values, transitions, gate, states, gain,
        scratch=[pltpu.VMEM((heads, D, D), BF16)],
    )
    with jax.named_scope("to_tokens"):
        other = lax.ppermute(send, "head", [(0, 1), (1, 0)])
    (out,) = call(
        kept_outputs, [((tokens // 2, 2 * heads * D), BF16, "hbm")],
        queries, keys, values, kept, gain,
        scratch=[pltpu.VMEM(half, BF16), pltpu.SemaphoreType.DMA(())],
    )
    there = (1 - lax.axis_index("head")) * (heads * D)
    return lax.dynamic_update_slice(out, other, (0, there))


def solution(mesh):
    placed = (
        P("seq", "head"),
        P("seq", "head"),
        P("seq", "head"),
        P("seq", "head", None, None),
        P("seq", "head"),
        P(),
    )
    return jax.shard_map(
        shards, mesh=mesh, in_specs=placed, out_specs=P(("seq", "head"), None), check_vma=False
    )
```

```python
import jax
import jax.numpy as jnp
from jax import lax
from jax.experimental import pallas as pl
from jax.experimental.pallas import tpu as pltpu
from jax.sharding import PartitionSpec as P

EPS = 1e-06
D = 128
ROWS = 2 * D
SCALE = 2.0**60
F32 = jnp.float32
BF16 = jnp.bfloat16
VMEM = pl.BlockSpec(memory_space=pltpu.VMEM)
PLAIN = pl.BlockSpec(memory_space=pltpu.VMEM)
ANY = pl.BlockSpec(memory_space=pl.ANY)


def dot(a, b, ca, cb):
    return lax.dot_general(a, b, (((ca,), (cb,)), ((), ())), preferred_element_type=F32)


def eye_mask():
    return lax.broadcasted_iota(jnp.int32, (D, D), 0) == lax.broadcasted_iota(
        jnp.int32, (D, D), 1
    )


def split(matrix, eye):
    matrix = matrix.astype(F32)
    row = jnp.sum(jnp.where(eye, matrix, 0.0), axis=0, keepdims=True)
    return row, jnp.where(eye, 0.0, matrix).astype(BF16)


def code(row):
    far = row * SCALE
    far = jnp.where(row < 0.0, jnp.minimum(far, -2.0), jnp.maximum(far, 2.0))
    return jnp.where((row >= 0.5) & (row <= 1.75), row - 1.0, far)


def decode(row):
    return jnp.where(jnp.abs(row) <= 1.0, row + 1.0, row * (1.0 / SCALE))


def pack(ref, at, both, eye):
    matrix = both[:D]
    row = jnp.sum(jnp.where(eye, matrix, 0.0), axis=0, keepdims=True)
    ref[(*at, pl.ds(0, D))] = jnp.where(eye, code(row), matrix).astype(BF16)
    ref[(*at, pl.ds(D, D))] = both[D:].astype(BF16)


def unpack(ref, at=()):
    row, rest = split(ref[(*at, pl.ds(0, D))], eye_mask())
    return decode(row), rest, ref[(*at, pl.ds(D, D))].astype(F32)


def dense(parts, eye):
    row, rest, state = parts
    return jnp.concatenate([jnp.where(eye, row, rest.astype(F32)), state], axis=0)


def divide(both, eye):
    return (*split(both[:D], eye), both[D:])


def then(both, parts):
    row, rest, state = parts
    after = both * row + dot(both.astype(BF16), rest, 1, 0)
    return jnp.concatenate([after[:D], after[D:] + state], axis=0)


def advance(state, parts):
    row, rest, add = parts
    return state * row + dot(state.astype(BF16), rest, 1, 0) + add


def local_compose(
    trans_hbm, gate_hbm, key_hbm, value_hbm, wire_ref, trans_ref, gate_ref, key_ref, value_ref, sems
):
    heads = range(trans_ref.shape[1])
    rows = key_ref.shape[0] // 2
    pairs = (
        (gate_hbm, gate_ref),
        (key_hbm, key_ref),
        (value_hbm, value_ref),
        (trans_hbm, trans_ref),
    )
    copies = [pltpu.make_async_copy(*pair, sems.at[i]) for i, pair in enumerate(pairs)]
    for copy in copies:
        copy.start()
    eye = eye_mask()
    copies[1].wait()
    copies[2].wait()

    def update(c, h):
        here = (pl.ds(c * rows, rows), pl.ds(h * D, D))
        return dot(value_ref[here], key_ref[here], 0, 0)

    updates = [(update(0, h).astype(BF16), update(1, h)) for h in heads]
    copies[0].wait()
    copies[3].wait()
    for h in heads:
        first, second = updates[h]
        a1 = trans_ref[1, h]
        state = gate_ref[1, h] * dot(first, a1, 1, 1) + second
        matrix = (gate_ref[0, h] * gate_ref[1, h]) * dot(trans_ref[0, h], a1, 0, 1)
        pack(wire_ref, (h,), jnp.concatenate([matrix, state], axis=0), eye)


def line_total(wire_ref, total_ref):
    eye = eye_mask()
    count = wire_ref.shape[0]
    runs = [
        then(dense(unpack(wire_ref, (z,)), eye), unpack(wire_ref, (z + 1,)))
        for z in range(0, count, 2)
    ]
    while len(runs) > 1:
        runs = [then(runs[i], divide(runs[i + 1], eye)) for i in range(0, len(runs), 2)]
    pack(total_ref, (), runs[0], eye)


def line_before(wire_ref, gain_in_ref, gate_in_ref, pre_ref, gain_ref, gate_ref):
    gain_ref[...] = gain_in_ref[...]
    for h in range(gate_ref.shape[0]):
        gate_ref[pl.ds(h, 1)] = jnp.broadcast_to(gate_in_ref[0:1, h : h + 1], (1, D))
    eye = eye_mask()
    run = jnp.concatenate([eye.astype(F32), jnp.zeros((D, D), F32)], axis=0)
    for z in range(wire_ref.shape[0]):
        pack(pre_ref, (z,), run, eye)
        if z == 0:
            run = dense(unpack(wire_ref, (0,)), eye)
        elif z < wire_ref.shape[0] - 1:
            run = then(run, unpack(wire_ref, (z,)))


def sort_ring(stride, refs, sorted_ref):
    me = lax.rem(lax.axis_index("seq") // stride, 4)
    for d, ref in zip((0, 2, 3, 1), refs):
        sorted_ref[me ^ d] = ref[...]
    return me


def plane_total(own_ref, a_ref, b_ref, c_ref, total_ref, sorted_ref):
    eye = eye_mask()
    sort_ring(8, (own_ref, a_ref, b_ref, c_ref), sorted_ref)
    one = then(dense(unpack(sorted_ref, (0,)), eye), unpack(sorted_ref, (1,)))
    two = then(dense(unpack(sorted_ref, (2,)), eye), unpack(sorted_ref, (3,)))
    pack(total_ref, (), then(one, divide(two, eye)), eye)


def plane_before(own_ref, a_ref, b_ref, c_ref, pre_ref, sorted_ref):
    eye = eye_mask()
    me = sort_ring(8, (own_ref, a_ref, b_ref, c_ref), sorted_ref)
    before = jnp.concatenate([eye.astype(F32), jnp.zeros((D, D), F32)], axis=0)
    run = dense(unpack(sorted_ref, (0,)), eye)
    before = jnp.where(me == 1, run, before)
    for y in (1, 2):
        run = then(run, unpack(sorted_ref, (y,)))
        before = jnp.where(me == y + 1, run, before)
    pack(pre_ref, (), before, eye)


def enter_states(own_ref, a_ref, b_ref, c_ref, plane_ref, line_ref, state_ref, sorted_ref):
    me = sort_ring(32, (own_ref, a_ref, b_ref, c_ref), sorted_ref)
    run = sorted_ref[0, pl.ds(D, D)].astype(F32)
    before = jnp.where(me == 1, run, 0.0)
    for x in (1, 2):
        run = advance(run, unpack(sorted_ref, (x,)))
        before = jnp.where(me == x + 1, run, before)
    run = advance(before, unpack(plane_ref))
    for z in range(line_ref.shape[0]):
        state_ref[z] = advance(run, unpack(line_ref, (z,))).astype(BF16)


def normed_block(block, query_ref, key_ref, value_ref, state_ref, gain_ref, out_ref):
    rows = key_ref.shape[0] // 2
    here = pl.ds(pl.multiple_of(block * rows, rows), rows)
    causal = lax.broadcasted_iota(jnp.int32, (rows, rows), 0) >= lax.broadcasted_iota(
        jnp.int32, (rows, rows), 1
    )
    gain = gain_ref[...]
    heads = range(state_ref.shape[0])
    cols = [pl.ds(h * D, D) for h in heads]
    scores = [dot(query_ref[here, c], key_ref[here, c], 1, 1) for c in cols]
    weights = [jnp.where(causal, x, 0.0).astype(BF16) for x in scores]
    mixed = [
        dot(query_ref[here, c], state_ref[h], 1, 1) + dot(w, value_ref[here, c], 1, 0)
        for h, c, w in zip(heads, cols, weights)
    ]
    for h in heads:
        mean = jnp.mean(mixed[h] * mixed[h], axis=-1, keepdims=True)
        out_ref(h, (mixed[h] * lax.rsqrt(mean + EPS) * gain).astype(BF16))


def sent_outputs(
    query_ref, key_ref, value_ref, trans_ref, gate_ref, state_ref, gain_ref,
    send_ref, kept_ref, used_ref,
):
    rows = key_ref.shape[0] // 2
    me = lax.axis_index("head")
    for h in range(state_ref.shape[0]):
        cols = pl.ds(h * D, D)
        entering = state_ref[h]
        upd = dot(value_ref[pl.ds(0, rows), cols], key_ref[pl.ds(0, rows), cols], 0, 0)
        later = gate_ref[pl.ds(h, 1)] * dot(entering, trans_ref[0, h], 1, 1) + upd
        first = entering.astype(F32)
        used_ref[h] = jnp.where(me == 0, later, first).astype(BF16)
        kept_ref[h] = jnp.where(me == 0, first, later).astype(BF16)

    def write(h, value):
        send_ref[:, pl.ds(h * D, D)] = value

    normed_block(1 - me, query_ref, key_ref, value_ref, used_ref, gain_ref, write)


def kept_outputs(query_ref, key_ref, value_ref, state_ref, gain_ref, out_hbm, half_ref, sem):
    me = lax.axis_index("head")
    width = half_ref.shape[1]

    def write(h, value):
        half_ref[:, pl.ds(h * D, D)] = value

    normed_block(me, query_ref, key_ref, value_ref, state_ref, gain_ref, write)
    here = pl.ds(pl.multiple_of(me * width, width), width)
    copy = pltpu.make_async_copy(half_ref, out_hbm.at[:, here], sem)
    copy.start()
    copy.wait()


def call(kernel, outs, *operands, scratch=(), flops=0, specs=None):
    shapes = [
        jax.ShapeDtypeStruct(*out[:2]) if len(out) > 2 else pltpu.VMEM(*out) for out in outs
    ]
    specs = specs or [VMEM] * len(operands)
    operands = [
        pltpu.with_memory_space_constraint(x, pltpu.VMEM) if spec is VMEM else x
        for x, spec in zip(operands, specs)
    ]
    return pl.pallas_call(
        kernel,
        out_shape=shapes,
        in_specs=specs,
        out_specs=[ANY if len(out) > 2 else VMEM for out in outs],
        scratch_shapes=scratch,
        cost_estimate=pl.CostEstimate(flops=flops, bytes_accessed=1 << 20, transcendentals=0),
        name=kernel.__name__,
    )(*operands)


def shards(queries, keys, values, transitions, gates, norm_gain):
    heads = transitions.shape[1]
    count = lax.axis_size("seq")
    tokens = queries.shape[0]
    lines = [[g * 8 + z for z in range(8)] for g in range(count // 8)]
    line = ((heads, ROWS, D), BF16)
    one = ((ROWS, D), BF16)
    ring = [pltpu.VMEM((4, ROWS, D), BF16)]

    def around(total, stride):
        out = []
        for d in (2, 3, 1):
            pairs = []
            for s in range(count):
                at = s // stride % 4
                pairs.append((s, s + ((at ^ d) - at) * stride))
            out.append(lax.ppermute(total, "seq", pairs))
        return lax.optimization_barrier(out)

    (wire,) = call(
        local_compose, [line], transitions, gates, keys, values, specs=[ANY] * 4,
        scratch=[
            pltpu.VMEM(transitions.shape, BF16),
            pltpu.SMEM(gates.shape, F32),
            pltpu.VMEM(keys.shape, BF16),
            pltpu.VMEM(values.shape, BF16),
            pltpu.SemaphoreType.DMA((4,)),
        ],
    )
    with jax.named_scope("to_owners"):
        wire = lax.all_to_all(wire, "seq", 0, 0, axis_index_groups=lines, tiled=True)
    (total,) = call(line_total, [one], wire)
    with jax.named_scope("along_y"):
        others = around(total, 8)
    line_pre, gain, gate = call(
        line_before, [line, ((1, D), F32), ((heads, D), F32)],
        wire, norm_gain.reshape(1, D), gates, specs=[VMEM, PLAIN, PLAIN],
    )
    (whole,) = call(plane_total, [one], total, *others, scratch=ring)
    with jax.named_scope("along_x"):
        planes = around(whole, 32)
    (plane_pre,) = call(plane_before, [one], total, *others, scratch=ring)
    (states,) = call(
        enter_states, [((heads, D, D), BF16)], whole, *planes, plane_pre, line_pre, scratch=ring
    )
    with jax.named_scope("from_owners"):
        states = lax.all_to_all(states, "seq", 0, 0, axis_index_groups=lines, tiled=True)
    half = (tokens // 2, heads * D)
    send, kept = call(
        sent_outputs,
        [(half, BF16), ((heads, D, D), BF16)],
        queries, keys, values, transitions, gate, states, gain,
        scratch=[pltpu.VMEM((heads, D, D), BF16)],
    )
    with jax.named_scope("to_tokens"):
        other = lax.ppermute(send, "head", [(0, 1), (1, 0)])
    (out,) = call(
        kept_outputs, [((tokens // 2, 2 * heads * D), BF16, "hbm")],
        queries, keys, values, kept, gain,
        scratch=[pltpu.VMEM(half, BF16), pltpu.SemaphoreType.DMA(())],
    )
    there = (1 - lax.axis_index("head")) * (heads * D)
    return lax.dynamic_update_slice(out, other, (0, there))


def solution(mesh):
    placed = (
        P("seq", "head"),
        P("seq", "head"),
        P("seq", "head"),
        P("seq", "head", None, None),
        P("seq", "head"),
        P(),
    )
    return jax.shard_map(
        shards, mesh=mesh, in_specs=placed, out_specs=P(("seq", "head"), None), check_vma=False
    )
```

```python
import jax
import jax.numpy as jnp
from jax import lax
from jax.experimental import pallas as pl
from jax.experimental.pallas import tpu as pltpu
from jax.sharding import PartitionSpec as P

EPS = 1e-06
ORDER = (2, 3, 1, 5, 6, 7, 4)
D = 128
ROWS = 2 * D
SCALE = 2.0**60
F32 = jnp.float32
BF16 = jnp.bfloat16
VMEM = pl.BlockSpec(memory_space=pltpu.VMEM)
PLAIN = pl.BlockSpec(memory_space=pltpu.VMEM)
ANY = pl.BlockSpec(memory_space=pl.ANY)


def dot(a, b, ca, cb):
    return lax.dot_general(a, b, (((ca,), (cb,)), ((), ())), preferred_element_type=F32)


def eye_mask():
    return lax.broadcasted_iota(jnp.int32, (D, D), 0) == lax.broadcasted_iota(
        jnp.int32, (D, D), 1
    )


def split(matrix, eye):
    matrix = matrix.astype(F32)
    row = jnp.sum(jnp.where(eye, matrix, 0.0), axis=0, keepdims=True)
    return row, jnp.where(eye, 0.0, matrix).astype(BF16)


def code(row):
    far = row * SCALE
    far = jnp.where(row < 0.0, jnp.minimum(far, -2.0), jnp.maximum(far, 2.0))
    return jnp.where((row >= 0.5) & (row <= 1.75), row - 1.0, far)


def decode(row):
    return jnp.where(jnp.abs(row) <= 1.0, row + 1.0, row * (1.0 / SCALE))


def pack(ref, at, both, eye):
    matrix = both[:D]
    row = jnp.sum(jnp.where(eye, matrix, 0.0), axis=0, keepdims=True)
    ref[(*at, pl.ds(0, D))] = jnp.where(eye, code(row), matrix).astype(BF16)
    ref[(*at, pl.ds(D, D))] = both[D:].astype(BF16)


def unpack(ref, at=()):
    row, rest = split(ref[(*at, pl.ds(0, D))], eye_mask())
    return decode(row), rest, ref[(*at, pl.ds(D, D))].astype(F32)


def dense(parts, eye):
    row, rest, state = parts
    return jnp.concatenate([jnp.where(eye, row, rest.astype(F32)), state], axis=0)


def divide(both, eye):
    return (*split(both[:D], eye), both[D:])


def then(both, parts):
    row, rest, state = parts
    after = both * row + dot(both.astype(BF16), rest, 1, 0)
    return jnp.concatenate([after[:D], after[D:] + state], axis=0)


def advance(state, parts):
    row, rest, add = parts
    return state * row + dot(state.astype(BF16), rest, 1, 0) + add


def local_compose(
    trans_hbm, gate_hbm, key_hbm, value_hbm, *refs
):
    *wires, trans_ref, gate_ref, key_ref, value_ref, sems = refs
    me = lax.rem(lax.axis_index("seq"), 8)
    heads = [me ^ d for d in range(trans_ref.shape[1])]
    rows = key_ref.shape[0] // 2
    pairs = (
        (gate_hbm, gate_ref),
        (key_hbm, key_ref),
        (value_hbm, value_ref),
        (trans_hbm, trans_ref),
    )
    copies = [pltpu.make_async_copy(*pair, sems.at[i]) for i, pair in enumerate(pairs)]
    for copy in copies:
        copy.start()
    eye = eye_mask()
    copies[1].wait()
    copies[2].wait()

    def update(c, h):
        here = (pl.ds(c * rows, rows), pl.ds(pl.multiple_of(h * D, D), D))
        return dot(value_ref[here], key_ref[here], 0, 0)

    updates = [(update(0, h).astype(BF16), update(1, h)) for h in heads]
    copies[0].wait()
    copies[3].wait()
    for d, h in enumerate(heads):
        first, second = updates[d]
        a1 = trans_ref[1, h]
        state = gate_ref[1, h] * dot(first, a1, 1, 1) + second
        matrix = (gate_ref[0, h] * gate_ref[1, h]) * dot(trans_ref[0, h], a1, 0, 1)
        pack(wires[d], (), jnp.concatenate([matrix, state], axis=0), eye)


def sort_line(refs, sorted_ref):
    me = lax.rem(lax.axis_index("seq"), 8)
    for d, ref in enumerate(refs):
        sorted_ref[me ^ d] = ref[...]


def line_total(*refs):
    *wires, total_ref, wire_ref = refs
    sort_line(wires, wire_ref)
    eye = eye_mask()
    count = wire_ref.shape[0]
    runs = [
        then(dense(unpack(wire_ref, (z,)), eye), unpack(wire_ref, (z + 1,)))
        for z in range(0, count, 2)
    ]
    while len(runs) > 1:
        runs = [then(runs[i], divide(runs[i + 1], eye)) for i in range(0, len(runs), 2)]
    pack(total_ref, (), runs[0], eye)


def line_before(*refs):
    *wires, gain_in_ref, gate_in_ref, pre_ref, gain_ref, gate_ref, wire_ref = refs
    sort_line(wires, wire_ref)
    gain_ref[...] = gain_in_ref[...]
    for h in range(gate_ref.shape[0]):
        gate_ref[pl.ds(h, 1)] = jnp.broadcast_to(gate_in_ref[0:1, h : h + 1], (1, D))
    eye = eye_mask()
    run = jnp.concatenate([eye.astype(F32), jnp.zeros((D, D), F32)], axis=0)
    for z in range(wire_ref.shape[0]):
        pack(pre_ref, (z,), run, eye)
        if z == 0:
            run = dense(unpack(wire_ref, (0,)), eye)
        elif z < wire_ref.shape[0] - 1:
            run = then(run, unpack(wire_ref, (z,)))


def sort_ring(stride, refs, sorted_ref):
    me = lax.rem(lax.axis_index("seq") // stride, 4)
    core = lax.axis_index("head")
    for d, ref in zip((0, 2 - core, 3, 1 + core), refs):
        sorted_ref[me ^ d] = ref[...]
    return me


def plane_total(own_ref, a_ref, b_ref, c_ref, total_ref, sorted_ref):
    eye = eye_mask()
    sort_ring(8, (own_ref, a_ref, b_ref, c_ref), sorted_ref)
    one = then(dense(unpack(sorted_ref, (0,)), eye), unpack(sorted_ref, (1,)))
    two = then(dense(unpack(sorted_ref, (2,)), eye), unpack(sorted_ref, (3,)))
    pack(total_ref, (), then(one, divide(two, eye)), eye)


def plane_before(own_ref, a_ref, b_ref, c_ref, pre_ref, sorted_ref):
    eye = eye_mask()
    me = sort_ring(8, (own_ref, a_ref, b_ref, c_ref), sorted_ref)
    before = jnp.concatenate([eye.astype(F32), jnp.zeros((D, D), F32)], axis=0)
    run = dense(unpack(sorted_ref, (0,)), eye)
    before = jnp.where(me == 1, run, before)
    for y in (1, 2):
        run = then(run, unpack(sorted_ref, (y,)))
        before = jnp.where(me == y + 1, run, before)
    pack(pre_ref, (), before, eye)


def enter_states(own_ref, a_ref, b_ref, c_ref, plane_ref, line_ref, state_ref, sorted_ref):
    me = sort_ring(32, (own_ref, a_ref, b_ref, c_ref), sorted_ref)
    run = sorted_ref[0, pl.ds(D, D)].astype(F32)
    before = jnp.where(me == 1, run, 0.0)
    for x in (1, 2):
        run = advance(run, unpack(sorted_ref, (x,)))
        before = jnp.where(me == x + 1, run, before)
    run = advance(before, unpack(plane_ref))
    for z in range(line_ref.shape[0]):
        state_ref[z] = advance(run, unpack(line_ref, (z,))).astype(BF16)


def normed_block(block, query_ref, key_ref, value_ref, state_ref, gain_ref, out_ref):
    rows = key_ref.shape[0] // 2
    here = pl.ds(pl.multiple_of(block * rows, rows), rows)
    causal = lax.broadcasted_iota(jnp.int32, (rows, rows), 0) >= lax.broadcasted_iota(
        jnp.int32, (rows, rows), 1
    )
    gain = gain_ref[...]
    heads = range(state_ref.shape[0])
    cols = [pl.ds(h * D, D) for h in heads]
    scores = [dot(query_ref[here, c], key_ref[here, c], 1, 1) for c in cols]
    weights = [jnp.where(causal, x, 0.0).astype(BF16) for x in scores]
    mixed = [
        dot(query_ref[here, c], state_ref[h], 1, 1) + dot(w, value_ref[here, c], 1, 0)
        for h, c, w in zip(heads, cols, weights)
    ]
    for h in heads:
        mean = jnp.mean(mixed[h] * mixed[h], axis=-1, keepdims=True)
        out_ref(h, (mixed[h] * lax.rsqrt(mean + EPS) * gain).astype(BF16))


def sent_outputs(
    query_ref, key_ref, value_ref, trans_ref, gate_ref, state_ref, gain_ref,
    send_ref, kept_ref, used_ref,
):
    rows = key_ref.shape[0] // 2
    me = lax.axis_index("head")
    for h in range(state_ref.shape[0]):
        cols = pl.ds(h * D, D)
        entering = state_ref[h]
        upd = dot(value_ref[pl.ds(0, rows), cols], key_ref[pl.ds(0, rows), cols], 0, 0)
        later = gate_ref[pl.ds(h, 1)] * dot(entering, trans_ref[0, h], 1, 1) + upd
        first = entering.astype(F32)
        used_ref[h] = jnp.where(me == 0, later, first).astype(BF16)
        kept_ref[h] = jnp.where(me == 0, first, later).astype(BF16)

    def write(h, value):
        send_ref[:, pl.ds(h * D, D)] = value

    normed_block(1 - me, query_ref, key_ref, value_ref, used_ref, gain_ref, write)


def kept_outputs(query_ref, key_ref, value_ref, state_ref, gain_ref, out_hbm, half_ref, sem):
    me = lax.axis_index("head")
    width = half_ref.shape[1]

    def write(h, value):
        half_ref[:, pl.ds(h * D, D)] = value

    normed_block(me, query_ref, key_ref, value_ref, state_ref, gain_ref, write)
    here = pl.ds(pl.multiple_of(me * width, width), width)
    copy = pltpu.make_async_copy(half_ref, out_hbm.at[:, here], sem)
    copy.start()
    copy.wait()


def call(kernel, outs, *operands, scratch=(), flops=0, specs=None):
    shapes = [
        jax.ShapeDtypeStruct(*out[:2]) if len(out) > 2 else pltpu.VMEM(*out) for out in outs
    ]
    specs = specs or [VMEM] * len(operands)
    operands = [
        pltpu.with_memory_space_constraint(x, pltpu.VMEM) if spec is VMEM else x
        for x, spec in zip(operands, specs)
    ]
    return pl.pallas_call(
        kernel,
        out_shape=shapes,
        in_specs=specs,
        out_specs=[ANY if len(out) > 2 else VMEM for out in outs],
        scratch_shapes=scratch,
        cost_estimate=pl.CostEstimate(flops=flops, bytes_accessed=1 << 20, transcendentals=0),
        name=kernel.__name__,
    )(*operands)


def shards(queries, keys, values, transitions, gates, norm_gain):
    heads = transitions.shape[1]
    count = lax.axis_size("seq")
    tokens = queries.shape[0]
    lines = [[g * 8 + z for z in range(8)] for g in range(count // 8)]
    line = ((heads, ROWS, D), BF16)
    one = ((ROWS, D), BF16)
    ring = [pltpu.VMEM((4, ROWS, D), BF16)]

    def around(total, stride):
        out = []
        for d in (2, 3, 1):
            pairs = []
            for s in range(count):
                at = s // stride % 4
                for core, e in ((0, d), (1, {2: 1, 3: 3, 1: 2}[d])):
                    pairs.append((2 * s + core, 2 * (s + ((at ^ e) - at) * stride) + core))
            out.append(lax.ppermute(total, ("seq", "head"), pairs))
        return lax.optimization_barrier(out)

    wires = call(
        local_compose, [one] * heads, transitions, gates, keys, values, specs=[ANY] * 4,
        scratch=[
            pltpu.VMEM(transitions.shape, BF16),
            pltpu.SMEM(gates.shape, F32),
            pltpu.VMEM(keys.shape, BF16),
            pltpu.VMEM(values.shape, BF16),
            pltpu.SemaphoreType.DMA((4,)),
        ],
    )
    with jax.named_scope("to_owners"):
        got = [
            lax.ppermute(wires[d], "seq", [(s, s ^ d) for s in range(count)]) for d in ORDER
        ]
        got = dict(zip(ORDER, lax.optimization_barrier(got)))
        wires = [wires[0]] + [got[d] for d in range(1, heads)]
    lined = [pltpu.VMEM(*line)]
    (total,) = call(line_total, [one], *wires, scratch=lined)
    with jax.named_scope("along_y"):
        others = around(total, 8)
    line_pre, gain, gate = call(
        line_before, [line, ((1, D), F32), ((heads, D), F32)],
        *wires, norm_gain.reshape(1, D), gates, specs=[VMEM] * heads + [PLAIN, PLAIN], scratch=lined,
    )
    (whole,) = call(plane_total, [one], total, *others, scratch=ring)
    with jax.named_scope("along_x"):
        planes = around(whole, 32)
    (plane_pre,) = call(plane_before, [one], total, *others, scratch=ring)
    (states,) = call(
        enter_states, [((heads, D, D), BF16)], whole, *planes, plane_pre, line_pre, scratch=ring
    )
    with jax.named_scope("from_owners"):
        states = lax.all_to_all(states, "seq", 0, 0, axis_index_groups=lines, tiled=True)
    half = (tokens // 2, heads * D)
    send, kept = call(
        sent_outputs,
        [(half, BF16), ((heads, D, D), BF16)],
        queries, keys, values, transitions, gate, states, gain,
        scratch=[pltpu.VMEM((heads, D, D), BF16)],
    )
    with jax.named_scope("to_tokens"):
        other = lax.ppermute(send, "head", [(0, 1), (1, 0)])
    (out,) = call(
        kept_outputs, [((tokens // 2, 2 * heads * D), BF16, "hbm")],
        queries, keys, values, kept, gain,
        scratch=[pltpu.VMEM(half, BF16), pltpu.SemaphoreType.DMA(())],
    )
    there = (1 - lax.axis_index("head")) * (heads * D)
    return lax.dynamic_update_slice(out, other, (0, there))


def solution(mesh):
    placed = (
        P("seq", "head"),
        P("seq", "head"),
        P("seq", "head"),
        P("seq", "head", None, None),
        P("seq", "head"),
        P(),
    )
    return jax.shard_map(
        shards, mesh=mesh, in_specs=placed, out_specs=P(("seq", "head"), None), check_vma=False
    )
```

```python
import jax
import jax.numpy as jnp
from jax import lax
from jax.experimental import pallas as pl
from jax.experimental.pallas import tpu as pltpu
from jax.sharding import PartitionSpec as P

EPS = 1e-06
ORDER = (2, 3, 1, 5, 6, 7, 4)
D = 128
ROWS = 2 * D
SCALE = 2.0**60
F32 = jnp.float32
BF16 = jnp.bfloat16
VMEM = pl.BlockSpec(memory_space=pltpu.VMEM)
PLAIN = pl.BlockSpec(memory_space=pltpu.VMEM)
ANY = pl.BlockSpec(memory_space=pl.ANY)


def dot(a, b, ca, cb):
    return lax.dot_general(a, b, (((ca,), (cb,)), ((), ())), preferred_element_type=F32)


def eye_mask():
    return lax.broadcasted_iota(jnp.int32, (D, D), 0) == lax.broadcasted_iota(
        jnp.int32, (D, D), 1
    )


def split(matrix, eye):
    matrix = matrix.astype(F32)
    row = jnp.sum(jnp.where(eye, matrix, 0.0), axis=0, keepdims=True)
    return row, jnp.where(eye, 0.0, matrix).astype(BF16)


def code(row):
    far = row * SCALE
    far = jnp.where(row < 0.0, jnp.minimum(far, -2.0), jnp.maximum(far, 2.0))
    return jnp.where((row >= 0.5) & (row <= 1.75), row - 1.0, far)


def decode(row):
    return jnp.where(jnp.abs(row) <= 1.0, row + 1.0, row * (1.0 / SCALE))


def pack(ref, at, both, eye):
    matrix = both[:D]
    row = jnp.sum(jnp.where(eye, matrix, 0.0), axis=0, keepdims=True)
    ref[(*at, pl.ds(0, D))] = jnp.where(eye, code(row), matrix).astype(BF16)
    ref[(*at, pl.ds(D, D))] = both[D:].astype(BF16)


def unpack(ref, at=()):
    row, rest = split(ref[(*at, pl.ds(0, D))], eye_mask())
    return decode(row), rest, ref[(*at, pl.ds(D, D))].astype(F32)


def dense(parts, eye):
    row, rest, state = parts
    return jnp.concatenate([jnp.where(eye, row, rest.astype(F32)), state], axis=0)


def divide(both, eye):
    return (*split(both[:D], eye), both[D:])


def then(both, parts):
    row, rest, state = parts
    after = both * row + dot(both.astype(BF16), rest, 1, 0)
    return jnp.concatenate([after[:D], after[D:] + state], axis=0)


def advance(state, parts):
    row, rest, add = parts
    return state * row + dot(state.astype(BF16), rest, 1, 0) + add


def local_compose(
    trans_hbm, gate_hbm, key_hbm, value_hbm, *refs
):
    *wires, trans_ref, gate_ref, key_ref, value_ref, sems = refs
    me = lax.rem(lax.axis_index("seq"), 8)
    heads = [me ^ d for d in range(trans_ref.shape[1])]
    rows = key_ref.shape[0] // 2
    pairs = (
        (gate_hbm, gate_ref),
        (key_hbm, key_ref),
        (value_hbm, value_ref),
        (trans_hbm, trans_ref),
    )
    copies = [pltpu.make_async_copy(*pair, sems.at[i]) for i, pair in enumerate(pairs)]
    for copy in copies:
        copy.start()
    eye = eye_mask()
    copies[1].wait()
    copies[2].wait()

    def update(c, h):
        here = (pl.ds(c * rows, rows), pl.ds(pl.multiple_of(h * D, D), D))
        return dot(value_ref[here], key_ref[here], 0, 0)

    updates = [(update(0, h).astype(BF16), update(1, h)) for h in heads]
    copies[0].wait()
    copies[3].wait()
    for d, h in enumerate(heads):
        first, second = updates[d]
        a1 = trans_ref[1, h]
        state = gate_ref[1, h] * dot(first, a1, 1, 1) + second
        matrix = (gate_ref[0, h] * gate_ref[1, h]) * dot(trans_ref[0, h], a1, 0, 1)
        pack(wires[d], (), jnp.concatenate([matrix, state], axis=0), eye)


def sort_line(refs, sorted_ref):
    me = lax.rem(lax.axis_index("seq"), 8)
    for d, ref in enumerate(refs):
        sorted_ref[me ^ d] = ref[...]


def line_total(*refs):
    *wires, total_ref, wire_ref = refs
    sort_line(wires, wire_ref)
    eye = eye_mask()
    count = wire_ref.shape[0]
    runs = [
        then(dense(unpack(wire_ref, (z,)), eye), unpack(wire_ref, (z + 1,)))
        for z in range(0, count, 2)
    ]
    while len(runs) > 1:
        runs = [then(runs[i], divide(runs[i + 1], eye)) for i in range(0, len(runs), 2)]
    pack(total_ref, (), runs[0], eye)


def line_before(*refs):
    *wires, gain_in_ref, gate_in_ref, pre_ref, gain_ref, gate_ref, wire_ref = refs
    sort_line(wires, wire_ref)
    gain_ref[...] = gain_in_ref[...]
    for h in range(gate_ref.shape[0]):
        gate_ref[pl.ds(h, 1)] = jnp.broadcast_to(gate_in_ref[0:1, h : h + 1], (1, D))
    eye = eye_mask()
    run = jnp.concatenate([eye.astype(F32), jnp.zeros((D, D), F32)], axis=0)
    for z in range(wire_ref.shape[0]):
        pack(pre_ref, (z,), run, eye)
        if z == 0:
            run = dense(unpack(wire_ref, (0,)), eye)
        elif z < wire_ref.shape[0] - 1:
            run = then(run, unpack(wire_ref, (z,)))


def sort_ring(stride, refs, sorted_ref):
    me = lax.rem(lax.axis_index("seq") // stride, 4)
    core = lax.axis_index("head")
    for d, ref in zip((0, 2 - core, 3, 1 + core), refs):
        sorted_ref[me ^ d] = ref[...]
    return me


def plane_total(own_ref, a_ref, b_ref, c_ref, total_ref, sorted_ref):
    eye = eye_mask()
    sort_ring(8, (own_ref, a_ref, b_ref, c_ref), sorted_ref)
    one = then(dense(unpack(sorted_ref, (0,)), eye), unpack(sorted_ref, (1,)))
    two = then(dense(unpack(sorted_ref, (2,)), eye), unpack(sorted_ref, (3,)))
    pack(total_ref, (), then(one, divide(two, eye)), eye)


def plane_before(own_ref, a_ref, b_ref, c_ref, pre_ref, sorted_ref):
    eye = eye_mask()
    me = sort_ring(8, (own_ref, a_ref, b_ref, c_ref), sorted_ref)
    before = jnp.concatenate([eye.astype(F32), jnp.zeros((D, D), F32)], axis=0)
    run = dense(unpack(sorted_ref, (0,)), eye)
    before = jnp.where(me == 1, run, before)
    for y in (1, 2):
        run = then(run, unpack(sorted_ref, (y,)))
        before = jnp.where(me == y + 1, run, before)
    pack(pre_ref, (), before, eye)


def enter_states(own_ref, a_ref, b_ref, c_ref, plane_ref, line_ref, state_ref, sorted_ref):
    me = sort_ring(32, (own_ref, a_ref, b_ref, c_ref), sorted_ref)
    run = sorted_ref[0, pl.ds(D, D)].astype(F32)
    before = jnp.where(me == 1, run, 0.0)
    for x in (1, 2):
        run = advance(run, unpack(sorted_ref, (x,)))
        before = jnp.where(me == x + 1, run, before)
    run = advance(before, unpack(plane_ref))
    for z in range(line_ref.shape[0]):
        state_ref[z] = advance(run, unpack(line_ref, (z,))).astype(BF16)


def normed_block(block, query_ref, key_ref, value_ref, state_ref, gain_ref, out_ref):
    rows = key_ref.shape[0] // 2
    here = pl.ds(pl.multiple_of(block * rows, rows), rows)
    causal = lax.broadcasted_iota(jnp.int32, (rows, rows), 0) >= lax.broadcasted_iota(
        jnp.int32, (rows, rows), 1
    )
    gain = gain_ref[...]
    heads = range(state_ref.shape[0])
    cols = [pl.ds(h * D, D) for h in heads]
    scores = [dot(query_ref[here, c], key_ref[here, c], 1, 1) for c in cols]
    weights = [jnp.where(causal, x, 0.0).astype(BF16) for x in scores]
    mixed = [
        dot(query_ref[here, c], state_ref[h], 1, 1) + dot(w, value_ref[here, c], 1, 0)
        for h, c, w in zip(heads, cols, weights)
    ]
    for h in heads:
        mean = jnp.mean(mixed[h] * mixed[h], axis=-1, keepdims=True)
        out_ref(h, (mixed[h] * lax.rsqrt(mean + EPS) * gain).astype(BF16))


def sent_outputs(
    query_ref, key_ref, value_ref, trans_ref, gate_ref, state_ref, gain_ref,
    send_ref, kept_ref, used_ref,
):
    rows = key_ref.shape[0] // 2
    me = lax.axis_index("head")
    for h in range(state_ref.shape[0]):
        cols = pl.ds(h * D, D)
        entering = state_ref[h]
        upd = dot(value_ref[pl.ds(0, rows), cols], key_ref[pl.ds(0, rows), cols], 0, 0)
        later = gate_ref[pl.ds(h, 1)] * dot(entering, trans_ref[0, h], 1, 1) + upd
        first = entering.astype(F32)
        used_ref[h] = jnp.where(me == 0, later, first).astype(BF16)
        kept_ref[h] = jnp.where(me == 0, first, later).astype(BF16)

    def write(h, value):
        send_ref[:, pl.ds(h * D, D)] = value

    normed_block(1 - me, query_ref, key_ref, value_ref, used_ref, gain_ref, write)


def kept_outputs(query_ref, key_ref, value_ref, state_ref, gain_ref, out_hbm, half_ref, sem):
    me = lax.axis_index("head")
    width = half_ref.shape[1]

    def write(h, value):
        half_ref[:, pl.ds(h * D, D)] = value

    normed_block(me, query_ref, key_ref, value_ref, state_ref, gain_ref, write)
    here = pl.ds(pl.multiple_of(me * width, width), width)
    copy = pltpu.make_async_copy(half_ref, out_hbm.at[:, here], sem)
    copy.start()
    copy.wait()


def call(kernel, outs, *operands, scratch=(), flops=0, specs=None):
    shapes = [
        jax.ShapeDtypeStruct(*out[:2]) if len(out) > 2 else pltpu.VMEM(*out) for out in outs
    ]
    specs = specs or [VMEM] * len(operands)
    operands = [
        pltpu.with_memory_space_constraint(x, pltpu.VMEM) if spec is VMEM else x
        for x, spec in zip(operands, specs)
    ]
    return pl.pallas_call(
        kernel,
        out_shape=shapes,
        in_specs=specs,
        out_specs=[ANY if len(out) > 2 else VMEM for out in outs],
        scratch_shapes=scratch,
        cost_estimate=pl.CostEstimate(flops=flops, bytes_accessed=1 << 20, transcendentals=0),
        name=kernel.__name__,
    )(*operands)


def shards(queries, keys, values, transitions, gates, norm_gain):
    heads = transitions.shape[1]
    count = lax.axis_size("seq")
    tokens = queries.shape[0]
    lines = [[g * 8 + z for z in range(8)] for g in range(count // 8)]
    line = ((heads, ROWS, D), BF16)
    one = ((ROWS, D), BF16)
    ring = [pltpu.VMEM((4, ROWS, D), BF16)]

    def around(total, stride):
        out = []
        for d in (2, 3, 1):
            pairs = []
            for s in range(count):
                at = s // stride % 4
                for core, e in ((0, d), (1, {2: 1, 3: 3, 1: 2}[d])):
                    pairs.append((2 * s + core, 2 * (s + ((at ^ e) - at) * stride) + core))
            out.append(lax.ppermute(total, ("seq", "head"), pairs))
        return lax.optimization_barrier(out)

    wires = call(
        local_compose, [one] * heads, transitions, gates, keys, values, specs=[ANY] * 4,
        scratch=[
            pltpu.VMEM(transitions.shape, BF16),
            pltpu.SMEM(gates.shape, F32),
            pltpu.VMEM(keys.shape, BF16),
            pltpu.VMEM(values.shape, BF16),
            pltpu.SemaphoreType.DMA((4,)),
        ],
    )
    with jax.named_scope("to_owners"):
        got = [
            lax.ppermute(wires[d], "seq", [(s, s ^ d) for s in range(count)]) for d in ORDER
        ]
        got = dict(zip(ORDER, lax.optimization_barrier(got)))
        wires = [wires[0]] + [got[d] for d in range(1, heads)]
    lined = [pltpu.VMEM(*line)]
    (total,) = call(line_total, [one], *wires, scratch=lined)
    with jax.named_scope("along_y"):
        others = around(total, 8)
    line_pre, gain, gate = call(
        line_before, [line, ((1, D), F32), ((heads, D), F32)],
        *wires, norm_gain.reshape(1, D), gates, specs=[VMEM] * heads + [PLAIN, PLAIN], scratch=lined,
    )
    others, line_pre = lax.optimization_barrier((others, line_pre))
    (whole,) = call(plane_total, [one], total, *others, scratch=ring)
    with jax.named_scope("along_x"):
        planes = around(whole, 32)
    (plane_pre,) = call(plane_before, [one], total, *others, scratch=ring)
    (states,) = call(
        enter_states, [((heads, D, D), BF16)], whole, *planes, plane_pre, line_pre, scratch=ring
    )
    with jax.named_scope("from_owners"):
        states = lax.all_to_all(states, "seq", 0, 0, axis_index_groups=lines, tiled=True)
    half = (tokens // 2, heads * D)
    send, kept = call(
        sent_outputs,
        [(half, BF16), ((heads, D, D), BF16)],
        queries, keys, values, transitions, gate, states, gain,
        scratch=[pltpu.VMEM((heads, D, D), BF16)],
    )
    with jax.named_scope("to_tokens"):
        other = lax.ppermute(send, "head", [(0, 1), (1, 0)])
    (out,) = call(
        kept_outputs, [((tokens // 2, 2 * heads * D), BF16, "hbm")],
        queries, keys, values, kept, gain,
        scratch=[pltpu.VMEM(half, BF16), pltpu.SemaphoreType.DMA(())],
    )
    there = (1 - lax.axis_index("head")) * (heads * D)
    return lax.dynamic_update_slice(out, other, (0, there))


def solution(mesh):
    placed = (
        P("seq", "head"),
        P("seq", "head"),
        P("seq", "head"),
        P("seq", "head", None, None),
        P("seq", "head"),
        P(),
    )
    return jax.shard_map(
        shards, mesh=mesh, in_specs=placed, out_specs=P(("seq", "head"), None), check_vma=False
    )
```
